32 devices in a mesh: inline: 16 (over z, y, core), chan: 2 (over x).
Axes of the slice: x: 2, y: 2, z: 4, core: 2. Of those that a mesh axis runs over, the one named last changes fastest.
Arguments:
- inputs: bfloat16 [48, 4, 64, 256], P('inline', 'chan'), may hold values from -6 to 6
- w_in: bfloat16 [256, 256], replicated, may hold values from -0.375 to 0.375
- w_group: bfloat16 [27, 8, 256], replicated, may hold values from -0.4375 to 0.4375
- w_out: bfloat16 [256, 256], replicated, may hold values from -0.375 to 0.375
- cotangent: bfloat16 [48, 4, 64, 256], P('inline', 'chan'), may hold values from -6 to 6
Outputs:
- outputs: bfloat16 [48, 4, 64, 256], P('inline', 'chan')
- input_grad: bfloat16 [48, 4, 64, 256], P('inline', 'chan')
- grad_w_in: float32 [256, 256], replicated
- grad_group: float32 [27, 8, 256], replicated
- grad_w_out: float32 [256, 256], replicated
The draws below stay inside these ranges and needn't reach their ends.
All inputs are finite; a program needn't handle non-finite values.
Results may differ from the reference program's by a relative error of at most 0.0056.
Values may be sent and summed in bfloat16 or wider, within the bound.
A program may use at most 64 MiB of HBM per device.

```python
import jax
import jax.numpy as jnp

C = 256
GW = 8
DP = 64
IL = 48
XL = 4


def level_of(key, extent, pieces, smallest, top_value):
    def one(axis_at, shards_of):
        steps = jax.random.uniform(jax.random.fold_in(jax.random.fold_in(key, 6), axis_at), (shards_of,), jnp.float32, smallest / len(pieces), top_value / len(pieces))
        return jnp.repeat(jnp.exp(steps), extent[axis_at] // shards_of).reshape((-1,) + (1,) * (len(extent) - axis_at - 1))

    factor_of = one(*pieces[0])
    for cut in pieces[1:]:
        factor_of = factor_of * one(*cut)
    return factor_of


def noise(own_key, shape, scale, reach, split=(), kind=jnp.bfloat16):
    values = scale * jax.random.normal(own_key, shape, jnp.float32)
    if split:
        values = values * level_of(own_key, shape, split, -0.22, 0.18)
    return jnp.clip(values, -reach, reach).astype(kind)


def setup_inputs(seed: int = 0) -> dict:
    arg_keys = jax.random.split(jax.random.key(seed), 6)
    return {
        "inputs": noise(arg_keys[0], (IL, XL, DP, C), 1.0, 6.0, ((0, 16), (1, 2))),
        "w_in": noise(arg_keys[1], (C, C), C ** -0.5, 0.375),
        "w_group": noise(arg_keys[2], (27, GW, C), (27 * GW) ** -0.5, 0.4375),
        "w_out": noise(arg_keys[3], (C, C), C ** -0.5, 0.375),
        "cotangent": noise(arg_keys[4], (IL, XL, DP, C), 1.0, 6.0, ((0, 16), (1, 2))),
    }


def tap_offsets():
    return [(first, second, third) for first in range(3) for second in range(3) for third in range(3)]


def mixing(field, weight):
    flat = field.reshape(-1, field.shape[-1])
    return jnp.dot(flat, weight, preferred_element_type=jnp.float32).reshape(field.shape[:-1] + (weight.shape[1],))


def swish(value):
    return value * jax.nn.sigmoid(value)


def swish_slope(value):
    sig = jax.nn.sigmoid(value)
    return sig * (1.0 + value * (1.0 - sig))


def reference(inputs, w_in, w_group, w_out, cotangent):
    length, cross, depth, channels = inputs.shape
    groups_all = channels // GW
    cells = length * cross * depth
    pre_one = mixing(inputs, w_in)
    first = swish(pre_one).astype(jnp.bfloat16)
    volume_one = jnp.pad(first, ((1, 1), (1, 1), (1, 1), (0, 0)))
    conv = jnp.zeros((cells, groups_all, GW), jnp.float32)
    for index, (aa, bb, cc) in enumerate(tap_offsets()):
        window = volume_one[aa:aa + length, bb:bb + cross, cc:cc + depth].reshape(cells, groups_all, GW)
        kernel = w_group[index].reshape(GW, groups_all, GW).astype(jnp.float32)
        conv = conv + jnp.einsum("ngj,jgo->ngo", window.astype(jnp.float32), kernel)
    conv_flat = conv.reshape(cells, channels)
    second = swish(conv_flat).astype(jnp.bfloat16).reshape(length, cross, depth, channels)
    outputs = (inputs.astype(jnp.float32) + mixing(second, w_out)).astype(jnp.bfloat16)
    cot_flat = cotangent.reshape(cells, channels)
    second_flat = second.reshape(cells, channels)
    back_two = jnp.dot(cot_flat, w_out.T, preferred_element_type=jnp.float32)
    grad_w_out = jnp.dot(second_flat.T, cot_flat, preferred_element_type=jnp.float32)
    grad_conv = (back_two * swish_slope(conv_flat)).astype(jnp.bfloat16)
    volume_two = jnp.pad(grad_conv.reshape(length, cross, depth, channels), ((1, 1), (1, 1), (1, 1), (0, 0)))
    grad_split = grad_conv.reshape(cells, groups_all, GW).astype(jnp.float32)
    back_one = jnp.zeros((cells, groups_all, GW), jnp.float32)
    grads = []
    for index, (aa, bb, cc) in enumerate(tap_offsets()):
        kernel = w_group[index].reshape(GW, groups_all, GW).astype(jnp.float32)
        flipped = volume_two[2 - aa:2 - aa + length, 2 - bb:2 - bb + cross, 2 - cc:2 - cc + depth]
        flipped = flipped.reshape(cells, groups_all, GW).astype(jnp.float32)
        back_one = back_one + jnp.einsum("ngo,jgo->ngj", flipped, kernel)
        window = volume_one[aa:aa + length, bb:bb + cross, cc:cc + depth].reshape(cells, groups_all, GW)
        grads.append(jnp.einsum("ngj,ngo->jgo", window.astype(jnp.float32), grad_split).reshape(GW, channels))
    grad_group = jnp.stack(grads)
    pre_flat = pre_one.reshape(cells, channels)
    grad_mixed = (back_one.reshape(cells, channels) * swish_slope(pre_flat)).astype(jnp.bfloat16)
    back_in = jnp.dot(grad_mixed, w_in.T, preferred_element_type=jnp.float32)
    input_grad = (cot_flat.astype(jnp.float32) + back_in).astype(jnp.bfloat16).reshape(length, cross, depth, channels)
    grad_w_in = jnp.dot(inputs.reshape(cells, channels).T, grad_mixed, preferred_element_type=jnp.float32)
    return (outputs, input_grad, grad_w_in, grad_group, grad_w_out)
```

```python
import functools
import math

import jax
import jax.numpy as jnp
from jax import lax
from jax.experimental import pallas as pl
from jax.experimental.pallas import tpu as pltpu
from jax.sharding import PartitionSpec as P

GW = 8
BF = jnp.bfloat16
F32 = jnp.float32
MESH = pl.DeviceIdType.MESH
DIRS = [(di, dc) for di in (-1, 0, 1) for dc in (-1, 0, 1) if (di, dc) != (0, 0)]


def sigmoid(v):
    return jax.nn.sigmoid(v)


def dot_nn(a, b):
    return jnp.dot(a, b, preferred_element_type=F32)


def dot_nt(a, b):
    return lax.dot_general(a, b, (((1,), (1,)), ((), ())), preferred_element_type=F32)


def kernel(
    cfg,
    x_ref, win_ref, wg_ref, wout_ref, cot_ref,
    out_ref, ig_ref, gin_ref, ggr_ref, gout_ref,
    rx, ext, dfwd, dbwd, pre_s, back_s, gtap, part, recv1, recv2, fin,
    hs_sem, hr_sem, as_sem, ar_sem, bs_sem, br_sem, cs_sem, cr_sem,
):
    ni, nc, na_i, na_c = cfg
    na = na_i * na_c
    nb_c = nc // na_c
    nb = (ni // na_i) * nb_c
    rows, cross, depth, chans = x_ref.shape
    cells = rows * cross * depth
    i = lax.axis_index("inline")
    c = lax.axis_index("chan")
    ga = lax.rem(i, na_i) * na_c + lax.rem(c, na_c)
    gb = lax.div(i, na_i) * nb_c + lax.div(c, na_c)

    def peer_a(r):
        g = lax.rem(ga + r, na)
        return (
            lax.div(i, na_i) * na_i + lax.div(g, na_c),
            lax.div(c, na_c) * na_c + lax.rem(g, na_c),
        )

    def peer_b(r):
        g = lax.rem(gb + r, nb)
        return (
            lax.div(g, nb_c) * na_i + lax.rem(i, na_i),
            lax.rem(g, nb_c) * na_c + lax.rem(c, na_c),
        )

    def has(di, dc):
        ok = None
        for step, at, size in ((di, i, ni), (dc, c, nc)):
            if step:
                one = at < size - 1 if step > 0 else at > 0
                ok = one if ok is None else jnp.logical_and(ok, one)
        return ok

    def neighbour(di, dc):
        return (lax.rem(i + di + ni, ni), lax.rem(c + dc + nc, nc))

    for e in range(2):
        for p in (0, rows + 1):
            rx[e, p] = jnp.zeros((cross + 2, depth, chans), BF)
        for q in (0, cross + 1):
            rx[e, 1 : rows + 1, q] = jnp.zeros((rows, depth, chans), BF)

    barrier = pltpu.get_barrier_semaphore()
    count = jnp.int32(na - 1 + nb - 1)
    for d in DIRS:
        @pl.when(has(*d))
        def _():
            pl.semaphore_signal(barrier, inc=1, device_id=neighbour(*d), device_id_type=MESH)

        count = count + has(*d).astype(jnp.int32)
    for r in range(1, na):
        pl.semaphore_signal(barrier, inc=1, device_id=peer_a(r), device_id_type=MESH)
    for r in range(1, nb):
        pl.semaphore_signal(barrier, inc=1, device_id=peer_b(r), device_id_type=MESH)

    def halo(e, k):
        di, dc = DIRS[k]
        src_i = {1: rows, -1: 1, 0: pl.ds(1, rows)}[di]
        dst_i = {1: 0, -1: rows + 1, 0: pl.ds(1, rows)}[di]
        src_c = {1: cross, -1: 1, 0: pl.ds(1, cross)}[dc]
        dst_c = {1: 0, -1: cross + 1, 0: pl.ds(1, cross)}[dc]
        return pltpu.make_async_remote_copy(
            src_ref=rx.at[e, src_i, src_c],
            dst_ref=rx.at[e, dst_i, dst_c],
            send_sem=hs_sem.at[e, k],
            recv_sem=hr_sem.at[e, k],
            device_id=neighbour(di, dc),
            device_id_type=MESH,
        )

    def halo_start(e):
        for k, d in enumerate(DIRS):
            @pl.when(has(*d))
            def _():
                halo(e, k).start()

    def halo_wait(e):
        for k, d in enumerate(DIRS):
            @pl.when(has(-d[0], -d[1]))
            def _():
                halo(e, k).wait_recv()

    def halo_sent(e):
        for k, d in enumerate(DIRS):
            @pl.when(has(*d))
            def _():
                halo(e, k).wait_send()

    def shifted(e, p0, p1, q0, q1):
        n = (p1 - p0) * (q1 - q0) * depth
        v = rx[e, p0:p1, q0:q1].reshape(n, chans)
        f = v.astype(F32)
        at = lax.rem(lax.broadcasted_iota(jnp.int32, (n, chans), 0), depth)
        up = jnp.where(at == 0, 0.0, pltpu.roll(f, 1, 0)).astype(BF)
        down = jnp.where(at == depth - 1, 0.0, pltpu.roll(f, n - 1, 0)).astype(BF)
        shape = (p1 - p0, q1 - q0, depth, chans)
        for s, piece in enumerate((up, v, down)):
            ext[e, p0:p1, q0:q1, :, s * chans : (s + 1) * chans] = piece.reshape(shape)

    def shifted_inner(e):
        shifted(e, 1, rows + 1, 1, cross + 1)

    def shifted_edges(e):
        shifted(e, 0, 1, 0, cross + 2)
        shifted(e, rows + 1, rows + 2, 0, cross + 2)
        shifted(e, 1, rows + 1, 0, 1)
        shifted(e, 1, rows + 1, cross + 1, cross + 2)

    def window(e, a):
        return jnp.concatenate(
            [ext[e, a : a + rows, b : b + cross].reshape(cells, 3 * chans) for b in range(3)],
            axis=1,
        )

    def scatter(q, r):
        return pltpu.make_async_remote_copy(
            src_ref=part.at[q, lax.rem(ga + r, na)],
            dst_ref=recv1.at[q, r],
            send_sem=as_sem.at[q, r],
            recv_sem=ar_sem.at[q, r],
            device_id=peer_a(r),
            device_id_type=MESH,
        )

    def spread(q, r, slot):
        return pltpu.make_async_remote_copy(
            src_ref=recv2.at[q, gb],
            dst_ref=recv2.at[q, slot],
            send_sem=bs_sem.at[q, r],
            recv_sem=br_sem.at[q, r],
            device_id=peer_b(r),
            device_id_type=MESH,
        )

    def gather(q, r, slot):
        return pltpu.make_async_remote_copy(
            src_ref=fin.at[q, ga],
            dst_ref=fin.at[q, slot],
            send_sem=cs_sem.at[q, r],
            recv_sem=cr_sem.at[q, r],
            device_id=peer_a(r),
            device_id_type=MESH,
        )

    def sum_start(q, value):
        part[q] = value.astype(BF).reshape(na, chans // na, chans)
        for r in range(1, na):
            scatter(q, r).start()

    def sum_spread(q):
        for r in range(1, na):
            scatter(q, r).wait_recv()
        total = part[q, ga].astype(F32)
        for r in range(1, na):
            total = total + recv1[q, r].astype(F32)
        recv2[q, gb] = total.astype(BF)
        for r in range(1, nb):
            spread(q, r, gb).start()

    def sum_gather(q):
        for r in range(1, nb):
            spread(q, r, lax.rem(gb + nb - r, nb)).wait_recv()
        total = recv2[q, 0].astype(F32)
        for s in range(1, nb):
            total = total + recv2[q, s].astype(F32)
        fin[q, ga] = total.astype(BF)
        for r in range(1, na):
            gather(q, r, ga).start()

    def sum_done(q):
        for r in range(1, na):
            gather(q, r, lax.rem(ga + na - r, na)).wait_recv()
        return fin[q].astype(F32).reshape(chans, chans)

    def sum_sent(q):
        for r in range(1, na):
            scatter(q, r).wait_send()
        for r in range(1, nb):
            spread(q, r, gb).wait_send()
        for r in range(1, na):
            gather(q, r, ga).wait_send()

    full = (rows, cross, depth, chans)
    x = x_ref[...].reshape(cells, chans)
    pre = dot_nn(x, win_ref[...])
    pre_s[...] = pre
    rx[0, 1 : rows + 1, 1 : cross + 1] = (pre * sigmoid(pre)).astype(BF).reshape(full)
    pl.semaphore_wait(barrier, count)
    halo_start(0)

    same = lax.div(lax.broadcasted_iota(jnp.int32, (chans, chans), 0), GW) == lax.div(
        lax.broadcasted_iota(jnp.int32, (chans, chans), 1), GW
    )

    def build(a, carry):
        for u in range(9):
            w = wg_ref[a * 9 + u].astype(F32)
            tiled = jnp.broadcast_to(w[None], (chans // GW, GW, chans)).reshape(chans, chans)
            dense = jnp.where(same, tiled, 0.0).astype(BF)
            dfwd[a, u * chans : (u + 1) * chans, :] = dense
            dbwd[2 - a, :, (8 - u) * chans : (9 - u) * chans] = dense
        return carry

    lax.fori_loop(0, 3, build, 0)
    shifted_inner(0)
    back_s[...] = dot_nt(cot_ref[...].reshape(cells, chans), wout_ref[...])
    halo_wait(0)
    shifted_edges(0)

    conv = dot_nn(window(0, 0), dfwd[0])
    for a in (1, 2):
        conv = conv + dot_nn(window(0, a), dfwd[a])
    sig = sigmoid(conv)
    second = (conv * sig).astype(BF)
    grad_conv = (back_s[...] * (sig * (1.0 + conv * (1.0 - sig)))).astype(BF)
    rx[1, 1 : rows + 1, 1 : cross + 1] = grad_conv.reshape(full)
    halo_start(1)

    sum_start(0, dot_nn(second.T, cot_ref[...].reshape(cells, chans)))
    mixed = dot_nn(second, wout_ref[...])
    out_ref[...] = (x_ref[...].reshape(cells, chans).astype(F32) + mixed).astype(BF).reshape(full)
    shifted_inner(1)

    gtap[...] = jnp.zeros(gtap.shape, F32)

    def taps(b, carry):
        for s in range(3):
            block = ext[0, :, pl.ds(b, cross), :, s * chans : (s + 1) * chans]
            turned = block.reshape((rows + 2) * cross * depth, chans).T
            for a in range(3):
                begin = a * cross * depth
                g = dot_nn(
                    turned[:, begin : begin + cells],
                    rx[1, 1 : rows + 1, 1 : cross + 1].reshape(cells, chans),
                )
                g = jnp.where(same, g, 0.0).reshape(chans // GW, GW, chans)
                gtap[9 * a + 3 * b + s] = jnp.sum(g, axis=0)
        return carry

    lax.fori_loop(0, 3, taps, 0)
    sum_spread(0)
    sum_start(1, gtap[...].reshape(chans, chans))

    halo_wait(1)
    shifted_edges(1)
    back = dot_nt(window(1, 0), dbwd[0])
    for a in (1, 2):
        back = back + dot_nt(window(1, a), dbwd[a])
    sum_gather(0)
    sum_spread(1)
    pre = pre_s[...]
    sig = sigmoid(pre)
    mixed = (back * (sig * (1.0 + pre * (1.0 - sig)))).astype(BF)
    sum_start(2, dot_nn(x_ref[...].reshape(cells, chans).T, mixed))
    back_in = dot_nt(mixed, win_ref[...])
    cot32 = cot_ref[...].reshape(cells, chans).astype(F32)
    ig_ref[...] = (cot32 + back_in).astype(BF).reshape(full)
    sum_gather(1)
    sum_spread(2)
    gout_ref[...] = sum_done(0)
    sum_gather(2)
    ggr_ref[...] = sum_done(1)[: 27 * GW].reshape(27, GW, chans)
    gin_ref[...] = sum_done(2)
    for e in range(2):
        halo_sent(e)
    for q in range(3):
        sum_sent(q)


def shards(cfg, inputs, w_in, w_group, w_out, cotangent):
    ni, nc, na_i, na_c = cfg
    na = na_i * na_c
    nb = ni * nc // na
    rows, cross, depth, chans = inputs.shape
    cells = rows * cross * depth
    slab = (chans // na, chans)
    vmem = pl.BlockSpec(memory_space=pltpu.VMEM)
    dma = pltpu.SemaphoreType.DMA
    return pl.pallas_call(
        functools.partial(kernel, cfg),
        out_shape=(
            jax.ShapeDtypeStruct(inputs.shape, BF),
            jax.ShapeDtypeStruct(inputs.shape, BF),
            jax.ShapeDtypeStruct((chans, chans), F32),
            jax.ShapeDtypeStruct(w_group.shape, F32),
            jax.ShapeDtypeStruct((chans, chans), F32),
        ),
        in_specs=[vmem] * 5,
        out_specs=(vmem,) * 5,
        scratch_shapes=[
            pltpu.VMEM((2, rows + 2, cross + 2, depth, chans), BF),
            pltpu.VMEM((2, rows + 2, cross + 2, depth, 3 * chans), BF),
            pltpu.VMEM((3, 9 * chans, chans), BF),
            pltpu.VMEM((3, chans, 9 * chans), BF),
            pltpu.VMEM((cells, chans), F32),
            pltpu.VMEM((cells, chans), F32),
            pltpu.VMEM((chans // GW, GW, chans), F32),
            pltpu.VMEM((3, na) + slab, BF),
            pltpu.VMEM((3, na) + slab, BF),
            pltpu.VMEM((3, nb) + slab, BF),
            pltpu.VMEM((3, na) + slab, BF),
            dma((2, 8)),
            dma((2, 8)),
            dma((3, na)),
            dma((3, na)),
            dma((3, nb)),
            dma((3, nb)),
            dma((3, na)),
            dma((3, na)),
        ],
        compiler_params=pltpu.CompilerParams(
            collective_id=0, has_side_effects=True, vmem_limit_bytes=48 * 1024 * 1024
        ),
    )(inputs, w_in, w_group, w_out, cotangent)


def solution(mesh):
    ni, nc = mesh.shape["inline"], mesh.shape["chan"]
    cfg = (ni, nc, math.gcd(ni, 4), math.gcd(nc, 2))
    field = P("inline", "chan", None, None)
    return jax.shard_map(
        functools.partial(shards, cfg),
        mesh=mesh,
        in_specs=(field, P(), P(), P(), field),
        out_specs=(field, field, P(), P(), P()),
        check_vma=False,
    )
```

```python
import functools
import math

import jax
import jax.numpy as jnp
from jax import lax
from jax.experimental import pallas as pl
from jax.experimental.pallas import tpu as pltpu
from jax.sharding import PartitionSpec as P

GW = 8
BF = jnp.bfloat16
F32 = jnp.float32
MESH = pl.DeviceIdType.MESH
DIRS = [(di, dc) for di in (-1, 0, 1) for dc in (-1, 0, 1) if (di, dc) != (0, 0)]


def sigmoid(v):
    return jax.nn.sigmoid(v)


def dot_nn(a, b):
    return jnp.dot(a, b, preferred_element_type=F32)


def dot_nt(a, b):
    return lax.dot_general(a, b, (((1,), (1,)), ((), ())), preferred_element_type=F32)


def kernel(
    cfg,
    x_hbm, win_hbm, wg_hbm, wout_hbm, cot_hbm,
    out_ref, ig_ref, gin_ref, ggr_ref, gout_ref,
    x_ref, win_ref, wg_ref, wout_ref, cot_ref, in_sem,
    rx, ext, dfwd, dbwd, pre_s, back_s, gtap, *sums,
):
    part, recv1, recv2, fin = zip(sums[0:4], sums[4:8])
    hs_sem, hr_sem, as_sem, ar_sem, bs_sem, br_sem, cs_sem, cr_sem = sums[8:]
    fetch = [
        pltpu.make_async_copy(src, dst, in_sem.at[k])
        for k, (src, dst) in enumerate(
            (
                (x_hbm, x_ref),
                (win_hbm, win_ref),
                (wg_hbm, wg_ref),
                (wout_hbm, wout_ref),
                (cot_hbm, cot_ref),
            )
        )
    ]
    for one in fetch:
        one.start()
    ni, nc, na_i, na_c = cfg
    na = na_i * na_c
    nb_c = nc // na_c
    nb = (ni // na_i) * nb_c
    rows, cross, depth, chans = x_ref.shape
    cells = rows * cross * depth
    i = lax.axis_index("inline")
    c = lax.axis_index("chan")
    ga = lax.rem(i, na_i) * na_c + lax.rem(c, na_c)
    gb = lax.div(i, na_i) * nb_c + lax.div(c, na_c)

    def peer_a(r):
        g = lax.rem(ga + r, na)
        return (
            lax.div(i, na_i) * na_i + lax.div(g, na_c),
            lax.div(c, na_c) * na_c + lax.rem(g, na_c),
        )

    def peer_b(r):
        g = lax.rem(gb + r, nb)
        return (
            lax.div(g, nb_c) * na_i + lax.rem(i, na_i),
            lax.rem(g, nb_c) * na_c + lax.rem(c, na_c),
        )

    def has(di, dc):
        ok = None
        for step, at, size in ((di, i, ni), (dc, c, nc)):
            if step:
                one = at < size - 1 if step > 0 else at > 0
                ok = one if ok is None else jnp.logical_and(ok, one)
        return ok

    def neighbour(di, dc):
        return (lax.rem(i + di + ni, ni), lax.rem(c + dc + nc, nc))

    for e in range(2):
        for p in (0, rows + 1):
            rx[e, p] = jnp.zeros((cross + 2, depth, chans), BF)
        for q in (0, cross + 1):
            rx[e, 1 : rows + 1, q] = jnp.zeros((rows, depth, chans), BF)

    barrier = pltpu.get_barrier_semaphore()
    count = jnp.int32(na - 1 + nb - 1)
    for d in DIRS:
        @pl.when(has(*d))
        def _():
            pl.semaphore_signal(barrier, inc=1, device_id=neighbour(*d), device_id_type=MESH)

        count = count + has(*d).astype(jnp.int32)
    for r in range(1, na):
        pl.semaphore_signal(barrier, inc=1, device_id=peer_a(r), device_id_type=MESH)
    for r in range(1, nb):
        pl.semaphore_signal(barrier, inc=1, device_id=peer_b(r), device_id_type=MESH)

    def halo(e, k):
        di, dc = DIRS[k]
        src_i = {1: rows, -1: 1, 0: pl.ds(1, rows)}[di]
        dst_i = {1: 0, -1: rows + 1, 0: pl.ds(1, rows)}[di]
        src_c = {1: cross, -1: 1, 0: pl.ds(1, cross)}[dc]
        dst_c = {1: 0, -1: cross + 1, 0: pl.ds(1, cross)}[dc]
        return pltpu.make_async_remote_copy(
            src_ref=rx.at[e, src_i, src_c],
            dst_ref=rx.at[e, dst_i, dst_c],
            send_sem=hs_sem.at[e, k],
            recv_sem=hr_sem.at[e, k],
            device_id=neighbour(di, dc),
            device_id_type=MESH,
        )

    def halo_start(e):
        for k, d in enumerate(DIRS):
            @pl.when(has(*d))
            def _():
                halo(e, k).start()

    def halo_wait(e):
        for k, d in enumerate(DIRS):
            @pl.when(has(-d[0], -d[1]))
            def _():
                halo(e, k).wait_recv()

    def halo_sent(e):
        for k, d in enumerate(DIRS):
            @pl.when(has(*d))
            def _():
                halo(e, k).wait_send()

    def shifted(e, p0, p1, q0, q1):
        n = (p1 - p0) * (q1 - q0) * depth
        v = rx[e, p0:p1, q0:q1].reshape(n, chans)
        f = v.astype(F32)
        at = lax.rem(lax.broadcasted_iota(jnp.int32, (n, chans), 0), depth)
        up = jnp.where(at == 0, 0.0, pltpu.roll(f, 1, 0)).astype(BF)
        down = jnp.where(at == depth - 1, 0.0, pltpu.roll(f, n - 1, 0)).astype(BF)
        shape = (p1 - p0, q1 - q0, depth, chans)
        for s, piece in enumerate((up, v, down)):
            ext[e, p0:p1, q0:q1, :, s * chans : (s + 1) * chans] = piece.reshape(shape)

    def shifted_inner(e):
        shifted(e, 1, rows + 1, 1, cross + 1)

    def shifted_edges(e):
        shifted(e, 0, 1, 0, cross + 2)
        shifted(e, rows + 1, rows + 2, 0, cross + 2)
        shifted(e, 1, rows + 1, 0, 1)
        shifted(e, 1, rows + 1, cross + 1, cross + 2)

    def window(e, a):
        return jnp.concatenate(
            [ext[e, a : a + rows, b : b + cross].reshape(cells, 3 * chans) for b in range(3)],
            axis=1,
        )

    def scatter(q, r):
        return pltpu.make_async_remote_copy(
            src_ref=part[q].at[lax.rem(ga + r, na)],
            dst_ref=recv1[q].at[r],
            send_sem=as_sem.at[q, r],
            recv_sem=ar_sem.at[q, r],
            device_id=peer_a(r),
            device_id_type=MESH,
        )

    def spread(q, r, slot):
        return pltpu.make_async_remote_copy(
            src_ref=recv2[q].at[gb],
            dst_ref=recv2[q].at[slot],
            send_sem=bs_sem.at[q, r],
            recv_sem=br_sem.at[q, r],
            device_id=peer_b(r),
            device_id_type=MESH,
        )

    def gather(q, r, slot):
        return pltpu.make_async_remote_copy(
            src_ref=fin[q].at[ga],
            dst_ref=fin[q].at[slot],
            send_sem=cs_sem.at[q, r],
            recv_sem=cr_sem.at[q, r],
            device_id=peer_a(r),
            device_id_type=MESH,
        )

    def sum_start(q, *values):
        for k, value in enumerate(values):
            step = chans // na
            part[q][:, k * step : (k + 1) * step] = value.astype(BF).reshape(na, step, chans)
        for r in range(1, na):
            scatter(q, r).start()

    def sum_spread(q):
        for r in range(1, na):
            scatter(q, r).wait_recv()
        total = part[q][ga].astype(F32)
        for r in range(1, na):
            total = total + recv1[q][r].astype(F32)
        recv2[q][gb] = total.astype(BF)
        for r in range(1, nb):
            spread(q, r, gb).start()

    def sum_gather(q):
        for r in range(1, nb):
            spread(q, r, lax.rem(gb + nb - r, nb)).wait_recv()
        total = recv2[q][0].astype(F32)
        for s in range(1, nb):
            total = total + recv2[q][s].astype(F32)
        fin[q][ga] = total.astype(BF)
        for r in range(1, na):
            gather(q, r, ga).start()

    def sum_done(q):
        for r in range(1, na):
            gather(q, r, lax.rem(ga + na - r, na)).wait_recv()
        step = chans // na
        return [
            fin[q][:, k * step : (k + 1) * step].astype(F32).reshape(chans, chans)
            for k in range(fin[q].shape[1] // step)
        ]

    def sum_sent(q):
        for r in range(1, na):
            scatter(q, r).wait_send()
        for r in range(1, nb):
            spread(q, r, gb).wait_send()
        for r in range(1, na):
            gather(q, r, ga).wait_send()

    full = (rows, cross, depth, chans)
    fetch[0].wait()
    fetch[1].wait()
    x = x_ref[...].reshape(cells, chans)
    pre = dot_nn(x, win_ref[...])
    pre_s[...] = pre
    rx[0, 1 : rows + 1, 1 : cross + 1] = (pre * sigmoid(pre)).astype(BF).reshape(full)
    pl.semaphore_wait(barrier, count)
    halo_start(0)

    same = lax.div(lax.broadcasted_iota(jnp.int32, (chans, chans), 0), GW) == lax.div(
        lax.broadcasted_iota(jnp.int32, (chans, chans), 1), GW
    )

    def build(a, carry):
        for u in range(9):
            w = wg_ref[a * 9 + u].astype(F32)
            tiled = jnp.broadcast_to(w[None], (chans // GW, GW, chans)).reshape(chans, chans)
            dense = jnp.where(same, tiled, 0.0).astype(BF)
            dfwd[a, u * chans : (u + 1) * chans, :] = dense
            dbwd[2 - a, :, (8 - u) * chans : (9 - u) * chans] = dense
        return carry

    fetch[2].wait()
    lax.fori_loop(0, 3, build, 0)
    shifted_inner(0)
    fetch[3].wait()
    fetch[4].wait()
    back_s[...] = dot_nt(cot_ref[...].reshape(cells, chans), wout_ref[...])
    halo_wait(0)
    shifted_edges(0)

    conv = dot_nn(window(0, 0), dfwd[0])
    for a in (1, 2):
        conv = conv + dot_nn(window(0, a), dfwd[a])
    sig = sigmoid(conv)
    second = (conv * sig).astype(BF)
    grad_conv = (back_s[...] * (sig * (1.0 + conv * (1.0 - sig)))).astype(BF)
    rx[1, 1 : rows + 1, 1 : cross + 1] = grad_conv.reshape(full)
    halo_start(1)

    grad_out = dot_nn(second.T, cot_ref[...].reshape(cells, chans))
    back_s[0:chans] = grad_out
    mixed = dot_nn(second, wout_ref[...])
    out_ref[...] = (x_ref[...].reshape(cells, chans).astype(F32) + mixed).astype(BF).reshape(full)
    shifted_inner(1)

    gtap[...] = jnp.zeros(gtap.shape, F32)

    def taps(b, carry):
        for s in range(3):
            block = ext[0, :, pl.ds(b, cross), :, s * chans : (s + 1) * chans]
            turned = block.reshape((rows + 2) * cross * depth, chans).T
            for a in range(3):
                begin = a * cross * depth
                g = dot_nn(
                    turned[:, begin : begin + cells],
                    rx[1, 1 : rows + 1, 1 : cross + 1].reshape(cells, chans),
                )
                g = jnp.where(same, g, 0.0).reshape(chans // GW, GW, chans)
                gtap[9 * a + 3 * b + s] = jnp.sum(g, axis=0)
        return carry

    lax.fori_loop(0, 3, taps, 0)
    sum_start(0, back_s[0:chans], gtap[...].reshape(chans, chans))

    halo_wait(1)
    shifted_edges(1)
    back = dot_nt(window(1, 0), dbwd[0])
    for a in (1, 2):
        back = back + dot_nt(window(1, a), dbwd[a])
    sum_spread(0)
    pre = pre_s[...]
    sig = sigmoid(pre)
    mixed = (back * (sig * (1.0 + pre * (1.0 - sig)))).astype(BF)
    sum_start(1, dot_nn(x_ref[...].reshape(cells, chans).T, mixed))
    back_in = dot_nt(mixed, win_ref[...])
    cot32 = cot_ref[...].reshape(cells, chans).astype(F32)
    ig_ref[...] = (cot32 + back_in).astype(BF).reshape(full)
    sum_gather(0)
    sum_spread(1)
    gout_ref[...], group = sum_done(0)
    ggr_ref[...] = group[: 27 * GW].reshape(27, GW, chans)
    sum_gather(1)
    (gin_ref[...],) = sum_done(1)
    for e in range(2):
        halo_sent(e)
    for q in range(2):
        sum_sent(q)


def store(*refs):
    sem = refs[-1]
    copies = [pltpu.make_async_copy(refs[k], refs[5 + k], sem.at[k]) for k in range(5)]
    for one in copies:
        one.start()
    for one in copies:
        one.wait()


def shards(cfg, inputs, w_in, w_group, w_out, cotangent):
    ni, nc, na_i, na_c = cfg
    na = na_i * na_c
    nb = ni * nc // na
    rows, cross, depth, chans = inputs.shape
    cells = rows * cross * depth
    slab = (chans // na, chans)
    vmem = pl.BlockSpec(memory_space=pltpu.VMEM)
    dma = pltpu.SemaphoreType.DMA
    results = pl.pallas_call(
        functools.partial(kernel, cfg),
        out_shape=(
            jax.ShapeDtypeStruct(inputs.shape, BF),
            jax.ShapeDtypeStruct(inputs.shape, BF),
            jax.ShapeDtypeStruct((chans, chans), F32),
            jax.ShapeDtypeStruct(w_group.shape, F32),
            jax.ShapeDtypeStruct((chans, chans), F32),
        ),
        in_specs=[pl.BlockSpec(memory_space=pltpu.HBM)] * 5,
        out_specs=(vmem,) * 5,
        scratch_shapes=[
            *(pltpu.VMEM(one.shape, BF) for one in (inputs, w_in, w_group, w_out, cotangent)),
            dma((5,)),
            pltpu.VMEM((2, rows + 2, cross + 2, depth, chans), BF),
            pltpu.VMEM((2, rows + 2, cross + 2, depth, 3 * chans), BF),
            pltpu.VMEM((3, 9 * chans, chans), BF),
            pltpu.VMEM((3, chans, 9 * chans), BF),
            pltpu.VMEM((cells, chans), F32),
            pltpu.VMEM((cells, chans), F32),
            pltpu.VMEM((chans // GW, GW, chans), F32),
            *(
                pltpu.VMEM((count, depth_of * slab[0], chans), BF)
                for depth_of in (2, 1)
                for count in (na, na, nb, na)
            ),
            dma((2, 8)),
            dma((2, 8)),
            dma((2, na)),
            dma((2, na)),
            dma((2, nb)),
            dma((2, nb)),
            dma((2, na)),
            dma((2, na)),
        ],
        compiler_params=pltpu.CompilerParams(
            collective_id=0, has_side_effects=True, vmem_limit_bytes=64137 * 1024
        ),
    )(inputs, w_in, w_group, w_out, cotangent)
    return pl.pallas_call(
        store,
        out_shape=tuple(jax.ShapeDtypeStruct(one.shape, one.dtype) for one in results),
        in_specs=[vmem] * 5,
        out_specs=(pl.BlockSpec(memory_space=pltpu.HBM),) * 5,
        scratch_shapes=[dma((5,))],
    )(*results)


def solution(mesh):
    ni, nc = mesh.shape["inline"], mesh.shape["chan"]
    cfg = (ni, nc, math.gcd(ni, 4), math.gcd(nc, 2))
    field = P("inline", "chan", None, None)
    return jax.shard_map(
        functools.partial(shards, cfg),
        mesh=mesh,
        in_specs=(field, P(), P(), P(), field),
        out_specs=(field, field, P(), P(), P()),
        check_vma=False,
    )
```

```python
import functools
import math

import jax
import jax.numpy as jnp
from jax import lax
from jax.experimental import pallas as pl
from jax.experimental.pallas import tpu as pltpu
from jax.sharding import PartitionSpec as P

GW = 8
BF = jnp.bfloat16
F32 = jnp.float32
MESH = pl.DeviceIdType.MESH
DIRS = [(di, dc) for di in (-1, 0, 1) for dc in (-1, 0, 1) if (di, dc) != (0, 0)]


def sigmoid(v):
    return jax.nn.sigmoid(v)


def dot_nn(a, b):
    return jnp.dot(a, b, preferred_element_type=F32)


def dot_nt(a, b):
    return lax.dot_general(a, b, (((1,), (1,)), ((), ())), preferred_element_type=F32)


def kernel(
    cfg,
    x_hbm, win_hbm, wg_hbm, wout_hbm, cot_hbm,
    out_hbm, ig_hbm, gin_hbm, ggr_hbm, gout_hbm,
    out_ref, ig_ref, gin_ref, ggr_ref, gout_ref, out_sem, turned_x,
    x_ref, win_ref, wg_ref, wout_ref, cot_ref, in_sem,
    rx, ext, dfwd, dbwd, pre_s, back_s, gtap, *sums,
):
    part, recv1, recv2, fin = zip(sums[0:4], sums[4:8])
    hs_sem, hr_sem, as_sem, ar_sem, bs_sem, br_sem, cs_sem, cr_sem = sums[8:]
    fetch = [
        pltpu.make_async_copy(src, dst, in_sem.at[k])
        for k, (src, dst) in enumerate(
            (
                (x_hbm, x_ref),
                (win_hbm, win_ref),
                (wg_hbm, wg_ref),
                (wout_hbm, wout_ref),
                (cot_hbm, cot_ref),
            )
        )
    ]
    keep = [
        pltpu.make_async_copy(src, dst, out_sem.at[k])
        for k, (src, dst) in enumerate(
            (
                (out_ref, out_hbm),
                (ig_ref, ig_hbm),
                (gin_ref, gin_hbm),
                (ggr_ref, ggr_hbm),
                (gout_ref, gout_hbm),
            )
        )
    ]
    for one in fetch:
        one.start()
    ni, nc, na_i, na_c = cfg
    na = na_i * na_c
    nb_c = nc // na_c
    nb = (ni // na_i) * nb_c
    rows, cross, depth, chans = x_ref.shape
    cells = rows * cross * depth
    i = lax.axis_index("inline")
    c = lax.axis_index("chan")
    ga = lax.rem(i, na_i) * na_c + lax.rem(c, na_c)
    gb = lax.div(i, na_i) * nb_c + lax.div(c, na_c)

    def peer_a(r):
        g = lax.rem(ga + r, na)
        return (
            lax.div(i, na_i) * na_i + lax.div(g, na_c),
            lax.div(c, na_c) * na_c + lax.rem(g, na_c),
        )

    def peer_b(r):
        g = lax.rem(gb + r, nb)
        return (
            lax.div(g, nb_c) * na_i + lax.rem(i, na_i),
            lax.rem(g, nb_c) * na_c + lax.rem(c, na_c),
        )

    def has(di, dc):
        ok = None
        for step, at, size in ((di, i, ni), (dc, c, nc)):
            if step:
                one = at < size - 1 if step > 0 else at > 0
                ok = one if ok is None else jnp.logical_and(ok, one)
        return ok

    def neighbour(di, dc):
        return (lax.rem(i + di + ni, ni), lax.rem(c + dc + nc, nc))

    for e in range(2):
        for p in (0, rows + 1):
            rx[e, p] = jnp.zeros((cross + 2, depth, chans), BF)
        for q in (0, cross + 1):
            rx[e, 1 : rows + 1, q] = jnp.zeros((rows, depth, chans), BF)

    barrier = pltpu.get_barrier_semaphore()
    count = jnp.int32(na - 1 + nb - 1)
    for d in DIRS:
        @pl.when(has(*d))
        def _():
            pl.semaphore_signal(barrier, inc=1, device_id=neighbour(*d), device_id_type=MESH)

        count = count + has(*d).astype(jnp.int32)
    for r in range(1, na):
        pl.semaphore_signal(barrier, inc=1, device_id=peer_a(r), device_id_type=MESH)
    for r in range(1, nb):
        pl.semaphore_signal(barrier, inc=1, device_id=peer_b(r), device_id_type=MESH)

    def halo(e, k):
        di, dc = DIRS[k]
        src_i = {1: rows, -1: 1, 0: pl.ds(1, rows)}[di]
        dst_i = {1: 0, -1: rows + 1, 0: pl.ds(1, rows)}[di]
        src_c = {1: cross, -1: 1, 0: pl.ds(1, cross)}[dc]
        dst_c = {1: 0, -1: cross + 1, 0: pl.ds(1, cross)}[dc]
        return pltpu.make_async_remote_copy(
            src_ref=rx.at[e, src_i, src_c],
            dst_ref=rx.at[e, dst_i, dst_c],
            send_sem=hs_sem.at[e, k],
            recv_sem=hr_sem.at[e, k],
            device_id=neighbour(di, dc),
            device_id_type=MESH,
        )

    def halo_start(e):
        for k, d in enumerate(DIRS):
            @pl.when(has(*d))
            def _():
                halo(e, k).start()

    def halo_wait(e):
        for k, d in enumerate(DIRS):
            @pl.when(has(-d[0], -d[1]))
            def _():
                halo(e, k).wait_recv()

    def halo_sent(e):
        for k, d in enumerate(DIRS):
            @pl.when(has(*d))
            def _():
                halo(e, k).wait_send()

    def shifted(e, p0, p1, q0, q1):
        n = (p1 - p0) * (q1 - q0) * depth
        v = rx[e, p0:p1, q0:q1].reshape(n, chans)
        f = v.astype(F32)
        at = lax.rem(lax.broadcasted_iota(jnp.int32, (n, chans), 0), depth)
        up = jnp.where(at == 0, 0.0, pltpu.roll(f, 1, 0)).astype(BF)
        down = jnp.where(at == depth - 1, 0.0, pltpu.roll(f, n - 1, 0)).astype(BF)
        shape = (p1 - p0, q1 - q0, depth, chans)
        for s, piece in enumerate((up, v, down)):
            ext[e, p0:p1, q0:q1, :, s * chans : (s + 1) * chans] = piece.reshape(shape)

    def shifted_inner(e):
        shifted(e, 1, rows + 1, 1, cross + 1)

    def shifted_edges(e):
        shifted(e, 0, 1, 0, cross + 2)
        shifted(e, rows + 1, rows + 2, 0, cross + 2)
        shifted(e, 1, rows + 1, 0, 1)
        shifted(e, 1, rows + 1, cross + 1, cross + 2)

    def window(e, a):
        return jnp.concatenate(
            [ext[e, a : a + rows, b : b + cross].reshape(cells, 3 * chans) for b in range(3)],
            axis=1,
        )

    def scatter(q, r):
        return pltpu.make_async_remote_copy(
            src_ref=part[q].at[lax.rem(ga + r, na)],
            dst_ref=recv1[q].at[r],
            send_sem=as_sem.at[q, r],
            recv_sem=ar_sem.at[q, r],
            device_id=peer_a(r),
            device_id_type=MESH,
        )

    def spread(q, r, slot):
        return pltpu.make_async_remote_copy(
            src_ref=recv2[q].at[gb],
            dst_ref=recv2[q].at[slot],
            send_sem=bs_sem.at[q, r],
            recv_sem=br_sem.at[q, r],
            device_id=peer_b(r),
            device_id_type=MESH,
        )

    def gather(q, r, slot):
        return pltpu.make_async_remote_copy(
            src_ref=fin[q].at[ga],
            dst_ref=fin[q].at[slot],
            send_sem=cs_sem.at[q, r],
            recv_sem=cr_sem.at[q, r],
            device_id=peer_a(r),
            device_id_type=MESH,
        )

    def sum_start(q, *values):
        for k, value in enumerate(values):
            step = chans // na
            part[q][:, k * step : (k + 1) * step] = value.astype(BF).reshape(na, step, chans)
        for r in range(1, na):
            scatter(q, r).start()

    def sum_spread(q):
        for r in range(1, na):
            scatter(q, r).wait_recv()
        total = part[q][ga].astype(F32)
        for r in range(1, na):
            total = total + recv1[q][r].astype(F32)
        recv2[q][gb] = total.astype(BF)
        for r in range(1, nb):
            spread(q, r, gb).start()

    def sum_gather(q):
        for r in range(1, nb):
            spread(q, r, lax.rem(gb + nb - r, nb)).wait_recv()
        total = recv2[q][0].astype(F32)
        for s in range(1, nb):
            total = total + recv2[q][s].astype(F32)
        fin[q][ga] = total.astype(BF)
        for r in range(1, na):
            gather(q, r, ga).start()

    def sum_done(q):
        for r in range(1, na):
            gather(q, r, lax.rem(ga + na - r, na)).wait_recv()
        step = chans // na
        return [
            fin[q][:, k * step : (k + 1) * step].astype(F32).reshape(chans, chans)
            for k in range(fin[q].shape[1] // step)
        ]

    def sum_sent(q):
        for r in range(1, na):
            scatter(q, r).wait_send()
        for r in range(1, nb):
            spread(q, r, gb).wait_send()
        for r in range(1, na):
            gather(q, r, ga).wait_send()

    full = (rows, cross, depth, chans)
    fetch[0].wait()
    fetch[1].wait()
    x = x_ref[...].reshape(cells, chans)
    pre = dot_nn(x, win_ref[...])
    pre_s[...] = pre
    rx[0, 1 : rows + 1, 1 : cross + 1] = (pre * sigmoid(pre)).astype(BF).reshape(full)
    pl.semaphore_wait(barrier, count)
    halo_start(0)

    same = lax.div(lax.broadcasted_iota(jnp.int32, (chans, chans), 0), GW) == lax.div(
        lax.broadcasted_iota(jnp.int32, (chans, chans), 1), GW
    )

    def build(a, carry):
        for u in range(9):
            w = wg_ref[a * 9 + u].astype(F32)
            tiled = jnp.broadcast_to(w[None], (chans // GW, GW, chans)).reshape(chans, chans)
            dense = jnp.where(same, tiled, 0.0).astype(BF)
            dfwd[a, u * chans : (u + 1) * chans, :] = dense
            dbwd[2 - a, :, (8 - u) * chans : (9 - u) * chans] = dense
        return carry

    fetch[2].wait()
    lax.fori_loop(0, 3, build, 0)
    shifted_inner(0)
    fetch[3].wait()
    fetch[4].wait()
    back_s[...] = dot_nt(cot_ref[...].reshape(cells, chans), wout_ref[...])
    turned_x[...] = x_ref[...].reshape(cells, chans).T
    halo_wait(0)
    shifted_edges(0)

    conv = dot_nn(window(0, 0), dfwd[0])
    for a in (1, 2):
        conv = conv + dot_nn(window(0, a), dfwd[a])
    sig = sigmoid(conv)
    second = (conv * sig).astype(BF)
    grad_conv = (back_s[...] * (sig * (1.0 + conv * (1.0 - sig)))).astype(BF)
    rx[1, 1 : rows + 1, 1 : cross + 1] = grad_conv.reshape(full)
    halo_start(1)

    grad_out = dot_nn(second.T, cot_ref[...].reshape(cells, chans))
    back_s[0:chans] = grad_out
    mixed = dot_nn(second, wout_ref[...])
    out_ref[...] = (x_ref[...].reshape(cells, chans).astype(F32) + mixed).astype(BF).reshape(full)
    shifted_inner(1)
    keep[0].start()

    gtap[...] = jnp.zeros(gtap.shape, F32)

    def taps(b, carry):
        for s in range(3):
            block = ext[0, :, pl.ds(b, cross), :, s * chans : (s + 1) * chans]
            turned = block.reshape((rows + 2) * cross * depth, chans).T
            for a in range(3):
                begin = a * cross * depth
                g = dot_nn(
                    turned[:, begin : begin + cells],
                    rx[1, 1 : rows + 1, 1 : cross + 1].reshape(cells, chans),
                )
                g = jnp.where(same, g, 0.0).reshape(chans // GW, GW, chans)
                gtap[9 * a + 3 * b + s] = jnp.sum(g, axis=0)
        return carry

    lax.fori_loop(0, 3, taps, 0)
    sum_start(0, back_s[0:chans], gtap[...].reshape(chans, chans))

    halo_wait(1)
    shifted_edges(1)
    back = dot_nt(window(1, 0), dbwd[0])
    for a in (1, 2):
        back = back + dot_nt(window(1, a), dbwd[a])
    pre = pre_s[...]
    sig = sigmoid(pre)
    mixed = (back * (sig * (1.0 + pre * (1.0 - sig)))).astype(BF)
    sum_start(1, dot_nn(turned_x[...], mixed))
    back_in = dot_nt(mixed, win_ref[...])
    cot32 = cot_ref[...].reshape(cells, chans).astype(F32)
    ig_ref[...] = (cot32 + back_in).astype(BF).reshape(full)
    sum_spread(0)
    keep[1].start()
    sum_spread(1)
    sum_gather(0)
    sum_gather(1)
    gout_ref[...], group = sum_done(0)
    ggr_ref[...] = group[: 27 * GW].reshape(27, GW, chans)
    keep[3].start()
    keep[4].start()
    (gin_ref[...],) = sum_done(1)
    keep[2].start()
    for e in range(2):
        halo_sent(e)
    for q in range(2):
        sum_sent(q)
    for one in keep:
        one.wait()


def store(*refs):
    before, after = refs[-2:]
    loads = [pltpu.make_async_copy(refs[k], refs[10 + k], before.at[k]) for k in range(5)]
    stores = [pltpu.make_async_copy(refs[10 + k], refs[5 + k], after.at[k]) for k in range(5)]
    for one in loads:
        one.start()
    for load, one in zip(loads, stores):
        load.wait()
        one.start()
    for one in stores:
        one.wait()


def shards(cfg, inputs, w_in, w_group, w_out, cotangent):
    ni, nc, na_i, na_c = cfg
    na = na_i * na_c
    nb = ni * nc // na
    rows, cross, depth, chans = inputs.shape
    cells = rows * cross * depth
    slab = (chans // na, chans)
    hbm = pl.BlockSpec(memory_space=pltpu.HBM)
    whole = ((inputs, BF), (inputs, BF), (w_in, F32), (w_group, F32), (w_out, F32))
    staged = [pltpu.VMEM(one.shape, kind) for one, kind in whole]
    dma = pltpu.SemaphoreType.DMA
    results = pl.pallas_call(
        functools.partial(kernel, cfg),
        out_shape=(
            jax.ShapeDtypeStruct(inputs.shape, BF),
            jax.ShapeDtypeStruct(inputs.shape, BF),
            jax.ShapeDtypeStruct((chans, chans), F32),
            jax.ShapeDtypeStruct(w_group.shape, F32),
            jax.ShapeDtypeStruct((chans, chans), F32),
        ),
        in_specs=[pl.BlockSpec(memory_space=pltpu.HBM)] * 5,
        out_specs=(hbm,) * 5,
        scratch_shapes=[
            *staged,
            dma((5,)),
            pltpu.VMEM((chans, cells), BF),
            *(pltpu.VMEM(one.shape, BF) for one in (inputs, w_in, w_group, w_out, cotangent)),
            dma((5,)),
            pltpu.VMEM((2, rows + 2, cross + 2, depth, chans), BF),
            pltpu.VMEM((2, rows + 2, cross + 2, depth, 3 * chans), BF),
            pltpu.VMEM((3, 9 * chans, chans), BF),
            pltpu.VMEM((3, chans, 9 * chans), BF),
            pltpu.VMEM((cells, chans), F32),
            pltpu.VMEM((cells, chans), F32),
            pltpu.VMEM((chans // GW, GW, chans), F32),
            *(
                pltpu.VMEM((count, depth_of * slab[0], chans), BF)
                for depth_of in (2, 1)
                for count in (na, na, nb, na)
            ),
            dma((2, 8)),
            dma((2, 8)),
            dma((2, na)),
            dma((2, na)),
            dma((2, nb)),
            dma((2, nb)),
            dma((2, na)),
            dma((2, na)),
        ],
        compiler_params=pltpu.CompilerParams(
            collective_id=0, has_side_effects=True, vmem_limit_bytes=64137 * 1024
        ),
    )(inputs, w_in, w_group, w_out, cotangent)
    return pl.pallas_call(
        store,
        out_shape=tuple(jax.ShapeDtypeStruct(one.shape, one.dtype) for one in results),
        in_specs=[hbm] * 5,
        out_specs=(pl.BlockSpec(memory_space=pltpu.HBM),) * 5,
        scratch_shapes=[*staged, dma((5,)), dma((5,))],
        compiler_params=pltpu.CompilerParams(vmem_limit_bytes=64137 * 1024),
    )(*results)


def solution(mesh):
    ni, nc = mesh.shape["inline"], mesh.shape["chan"]
    cfg = (ni, nc, math.gcd(ni, 4), math.gcd(nc, 2))
    field = P("inline", "chan", None, None)
    return jax.shard_map(
        functools.partial(shards, cfg),
        mesh=mesh,
        in_specs=(field, P(), P(), P(), field),
        out_specs=(field, field, P(), P(), P()),
        check_vma=False,
    )
```

```python
import functools
import math

import jax
import jax.numpy as jnp
from jax import lax
from jax.experimental import pallas as pl
from jax.experimental.pallas import tpu as pltpu
from jax.sharding import PartitionSpec as P

GW = 8
BF = jnp.bfloat16
F32 = jnp.float32
MESH = pl.DeviceIdType.MESH
DIRS = [(di, dc) for di in (-1, 0, 1) for dc in (-1, 0, 1) if (di, dc) != (0, 0)]


def sigmoid(v):
    return jax.nn.sigmoid(v)


def dot_nn(a, b):
    return jnp.dot(a, b, preferred_element_type=F32)


def dot_nt(a, b):
    return lax.dot_general(a, b, (((1,), (1,)), ((), ())), preferred_element_type=F32)


def kernel(
    cfg,
    x_hbm, win_hbm, wg_hbm, wout_hbm, cot_hbm,
    out_hbm, ig_hbm, gin_hbm, ggr_hbm, gout_hbm,
    out_ref, ig_ref, gin_ref, ggr_ref, gout_ref, out_sem, turned_x,
    x_ref, win_ref, wg_ref, wout_ref, cot_ref, in_sem,
    rx, ext, dfwd, dbwd, pre_s, back_s, gtap, *sums,
):
    part, recv1, recv2, fin = zip(sums[0:4], sums[4:8])
    hs_sem, hr_sem, as_sem, ar_sem, bs_sem, br_sem, cs_sem, cr_sem = sums[8:]
    fetch = [
        pltpu.make_async_copy(src, dst, in_sem.at[k])
        for k, (src, dst) in enumerate(
            (
                (x_hbm, x_ref),
                (win_hbm, win_ref),
                (wg_hbm, wg_ref),
                (wout_hbm, wout_ref),
                (cot_hbm, cot_ref),
            )
        )
    ]
    keep = [
        pltpu.make_async_copy(src, dst, out_sem.at[k])
        for k, (src, dst) in enumerate(
            (
                (out_ref, out_hbm),
                (ig_ref, ig_hbm),
                (gin_ref, gin_hbm),
                (ggr_ref, ggr_hbm),
                (gout_ref, gout_hbm),
            )
        )
    ]
    for one in fetch:
        one.start()
    ni, nc, na_i, na_c = cfg
    na = na_i * na_c
    nb_c = nc // na_c
    nb = (ni // na_i) * nb_c
    rows, cross, depth, chans = x_ref.shape
    cells = rows * cross * depth
    i = lax.axis_index("inline")
    c = lax.axis_index("chan")
    ga = lax.rem(i, na_i) * na_c + lax.rem(c, na_c)
    gb = lax.div(i, na_i) * nb_c + lax.div(c, na_c)

    def peer_a(r):
        g = lax.rem(ga + r, na)
        return (
            lax.div(i, na_i) * na_i + lax.div(g, na_c),
            lax.div(c, na_c) * na_c + lax.rem(g, na_c),
        )

    def peer_b(r):
        g = lax.rem(gb + r, nb)
        return (
            lax.div(g, nb_c) * na_i + lax.rem(i, na_i),
            lax.rem(g, nb_c) * na_c + lax.rem(c, na_c),
        )

    def has(di, dc):
        ok = None
        for step, at, size in ((di, i, ni), (dc, c, nc)):
            if step:
                one = at < size - 1 if step > 0 else at > 0
                ok = one if ok is None else jnp.logical_and(ok, one)
        return ok

    def neighbour(di, dc):
        return (lax.rem(i + di + ni, ni), lax.rem(c + dc + nc, nc))

    for e in range(2):
        for p in (0, rows + 1):
            rx[e, p] = jnp.zeros((cross + 2, depth, chans), BF)
        for q in (0, cross + 1):
            rx[e, 1 : rows + 1, q] = jnp.zeros((rows, depth, chans), BF)

    barrier = pltpu.get_barrier_semaphore()
    count = jnp.int32(na - 1 + nb - 1)
    for d in DIRS:
        @pl.when(has(*d))
        def _():
            pl.semaphore_signal(barrier, inc=1, device_id=neighbour(*d), device_id_type=MESH)

        count = count + has(*d).astype(jnp.int32)
    for r in range(1, na):
        pl.semaphore_signal(barrier, inc=1, device_id=peer_a(r), device_id_type=MESH)
    for r in range(1, nb):
        pl.semaphore_signal(barrier, inc=1, device_id=peer_b(r), device_id_type=MESH)

    def halo(e, k):
        di, dc = DIRS[k]
        src_i = {1: rows, -1: 1, 0: pl.ds(1, rows)}[di]
        dst_i = {1: 0, -1: rows + 1, 0: pl.ds(1, rows)}[di]
        src_c = {1: cross, -1: 1, 0: pl.ds(1, cross)}[dc]
        dst_c = {1: 0, -1: cross + 1, 0: pl.ds(1, cross)}[dc]
        return pltpu.make_async_remote_copy(
            src_ref=rx.at[e, src_i, src_c],
            dst_ref=rx.at[e, dst_i, dst_c],
            send_sem=hs_sem.at[e, k],
            recv_sem=hr_sem.at[e, k],
            device_id=neighbour(di, dc),
            device_id_type=MESH,
        )

    def halo_start(e):
        for k, d in enumerate(DIRS):
            @pl.when(has(*d))
            def _():
                halo(e, k).start()

    def halo_wait(e):
        for k, d in enumerate(DIRS):
            @pl.when(has(-d[0], -d[1]))
            def _():
                halo(e, k).wait_recv()

    def halo_sent(e):
        for k, d in enumerate(DIRS):
            @pl.when(has(*d))
            def _():
                halo(e, k).wait_send()

    def shifted(e, p0, p1, q0, q1):
        n = (p1 - p0) * (q1 - q0) * depth
        v = rx[e, p0:p1, q0:q1].reshape(n, chans)
        f = v.astype(F32)
        at = lax.rem(lax.broadcasted_iota(jnp.int32, (n, chans), 0), depth)
        up = jnp.where(at == 0, 0.0, pltpu.roll(f, 1, 0)).astype(BF)
        down = jnp.where(at == depth - 1, 0.0, pltpu.roll(f, n - 1, 0)).astype(BF)
        shape = (p1 - p0, q1 - q0, depth, chans)
        for s, piece in enumerate((up, v, down)):
            ext[e, p0:p1, q0:q1, :, s * chans : (s + 1) * chans] = piece.reshape(shape)

    def shifted_inner(e):
        shifted(e, 1, rows + 1, 1, cross + 1)

    def shifted_edges(e):
        shifted(e, 0, 1, 0, cross + 2)
        shifted(e, rows + 1, rows + 2, 0, cross + 2)
        shifted(e, 1, rows + 1, 0, 1)
        shifted(e, 1, rows + 1, cross + 1, cross + 2)

    def window(e, a):
        return jnp.concatenate(
            [ext[e, a : a + rows, b : b + cross].reshape(cells, 3 * chans) for b in range(3)],
            axis=1,
        )

    def scatter(q, r):
        return pltpu.make_async_remote_copy(
            src_ref=part[q].at[lax.rem(ga + r, na)],
            dst_ref=recv1[q].at[r],
            send_sem=as_sem.at[q, r],
            recv_sem=ar_sem.at[q, r],
            device_id=peer_a(r),
            device_id_type=MESH,
        )

    def spread(q, r, slot):
        return pltpu.make_async_remote_copy(
            src_ref=recv2[q].at[gb],
            dst_ref=recv2[q].at[slot],
            send_sem=bs_sem.at[q, r],
            recv_sem=br_sem.at[q, r],
            device_id=peer_b(r),
            device_id_type=MESH,
        )

    def gather(q, r, slot):
        return pltpu.make_async_remote_copy(
            src_ref=fin[q].at[ga],
            dst_ref=fin[q].at[slot],
            send_sem=cs_sem.at[q, r],
            recv_sem=cr_sem.at[q, r],
            device_id=peer_a(r),
            device_id_type=MESH,
        )

    def sum_start(q, *values):
        for k, value in enumerate(values):
            step = chans // na
            part[q][:, k * step : (k + 1) * step] = value.astype(BF).reshape(na, step, chans)
        for r in range(1, na):
            scatter(q, r).start()

    def sum_spread(q):
        for r in range(1, na):
            scatter(q, r).wait_recv()
        total = part[q][ga].astype(F32)
        for r in range(1, na):
            total = total + recv1[q][r].astype(F32)
        recv2[q][gb] = total.astype(BF)
        for r in range(1, nb):
            spread(q, r, gb).start()

    def sum_gather(q):
        for r in range(1, nb):
            spread(q, r, lax.rem(gb + nb - r, nb)).wait_recv()
        total = recv2[q][0].astype(F32)
        for s in range(1, nb):
            total = total + recv2[q][s].astype(F32)
        fin[q][ga] = total.astype(BF)
        for r in range(1, na):
            gather(q, r, ga).start()

    def sum_done(q):
        for r in range(1, na):
            gather(q, r, lax.rem(ga + na - r, na)).wait_recv()
        step = chans // na
        return [
            fin[q][:, k * step : (k + 1) * step].astype(F32).reshape(chans, chans)
            for k in range(fin[q].shape[1] // step)
        ]

    def sum_sent(q):
        for r in range(1, na):
            scatter(q, r).wait_send()
        for r in range(1, nb):
            spread(q, r, gb).wait_send()
        for r in range(1, na):
            gather(q, r, ga).wait_send()

    full = (rows, cross, depth, chans)
    fetch[0].wait()
    fetch[1].wait()
    x = x_ref[...].reshape(cells, chans)
    pre = dot_nn(x, win_ref[...])
    pre_s[...] = pre
    rx[0, 1 : rows + 1, 1 : cross + 1] = (pre * sigmoid(pre)).astype(BF).reshape(full)
    pl.semaphore_wait(barrier, count)
    halo_start(0)

    same = lax.div(lax.broadcasted_iota(jnp.int32, (chans, chans), 0), GW) == lax.div(
        lax.broadcasted_iota(jnp.int32, (chans, chans), 1), GW
    )

    def build(a, carry):
        for u in range(9):
            w = wg_ref[a * 9 + u].astype(F32)
            tiled = jnp.broadcast_to(w[None], (chans // GW, GW, chans)).reshape(chans, chans)
            dense = jnp.where(same, tiled, 0.0).astype(BF)
            dfwd[a, u * chans : (u + 1) * chans, :] = dense
            dbwd[2 - a, :, (8 - u) * chans : (9 - u) * chans] = dense
        return carry

    fetch[2].wait()
    lax.fori_loop(0, 3, build, 0)
    shifted_inner(0)
    fetch[3].wait()
    fetch[4].wait()
    back_s[...] = dot_nt(cot_ref[...].reshape(cells, chans), wout_ref[...])
    turned_x[...] = x_ref[...].reshape(cells, chans).T
    halo_wait(0)
    shifted_edges(0)

    conv = dot_nn(window(0, 0), dfwd[0])
    for a in (1, 2):
        conv = conv + dot_nn(window(0, a), dfwd[a])
    sig = sigmoid(conv)
    second = (conv * sig).astype(BF)
    grad_conv = (back_s[...] * (sig * (1.0 + conv * (1.0 - sig)))).astype(BF)
    rx[1, 1 : rows + 1, 1 : cross + 1] = grad_conv.reshape(full)
    halo_start(1)

    grad_out = dot_nn(second.T, cot_ref[...].reshape(cells, chans))
    back_s[0:chans] = grad_out

    gtap[...] = jnp.zeros(gtap.shape, F32)

    def taps(b, carry):
        for s in range(3):
            block = ext[0, :, pl.ds(b, cross), :, s * chans : (s + 1) * chans]
            turned = block.reshape((rows + 2) * cross * depth, chans).T
            for a in range(3):
                begin = a * cross * depth
                g = dot_nn(
                    turned[:, begin : begin + cells],
                    rx[1, 1 : rows + 1, 1 : cross + 1].reshape(cells, chans),
                )
                g = jnp.where(same, g, 0.0).reshape(chans // GW, GW, chans)
                gtap[9 * a + 3 * b + s] = jnp.sum(g, axis=0)
        return carry

    lax.fori_loop(0, 3, taps, 0)
    sum_start(0, back_s[0:chans], gtap[...].reshape(chans, chans))
    mixed = dot_nn(second, wout_ref[...])
    out_ref[...] = (x_ref[...].reshape(cells, chans).astype(F32) + mixed).astype(BF).reshape(full)
    shifted_inner(1)
    keep[0].start()

    halo_wait(1)
    shifted_edges(1)
    back = dot_nt(window(1, 0), dbwd[0])
    for a in (1, 2):
        back = back + dot_nt(window(1, a), dbwd[a])
    pre = pre_s[...]
    sig = sigmoid(pre)
    mixed = (back * (sig * (1.0 + pre * (1.0 - sig)))).astype(BF)
    sum_start(1, dot_nn(turned_x[...], mixed))
    sum_spread(0)
    back_in = dot_nt(mixed, win_ref[...])
    cot32 = cot_ref[...].reshape(cells, chans).astype(F32)
    ig_ref[...] = (cot32 + back_in).astype(BF).reshape(full)
    keep[1].start()
    sum_spread(1)
    sum_gather(0)
    sum_gather(1)
    gout_ref[...], group = sum_done(0)
    ggr_ref[...] = group[: 27 * GW].reshape(27, GW, chans)
    keep[3].start()
    keep[4].start()
    (gin_ref[...],) = sum_done(1)
    keep[2].start()
    for e in range(2):
        halo_sent(e)
    for q in range(2):
        sum_sent(q)
    for one in keep:
        one.wait()


def store(*refs):
    before, after = refs[-2:]
    loads = [pltpu.make_async_copy(refs[k], refs[10 + k], before.at[k]) for k in range(5)]
    stores = [pltpu.make_async_copy(refs[10 + k], refs[5 + k], after.at[k]) for k in range(5)]
    for one in loads:
        one.start()
    for load, one in zip(loads, stores):
        load.wait()
        one.start()
    for one in stores:
        one.wait()


def shards(cfg, inputs, w_in, w_group, w_out, cotangent):
    ni, nc, na_i, na_c = cfg
    na = na_i * na_c
    nb = ni * nc // na
    rows, cross, depth, chans = inputs.shape
    cells = rows * cross * depth
    slab = (chans // na, chans)
    hbm = pl.BlockSpec(memory_space=pltpu.HBM)
    whole = ((inputs, BF), (inputs, BF), (w_in, F32), (w_group, F32), (w_out, F32))
    staged = [pltpu.VMEM(one.shape, kind) for one, kind in whole]
    dma = pltpu.SemaphoreType.DMA
    results = pl.pallas_call(
        functools.partial(kernel, cfg),
        out_shape=(
            jax.ShapeDtypeStruct(inputs.shape, BF),
            jax.ShapeDtypeStruct(inputs.shape, BF),
            jax.ShapeDtypeStruct((chans, chans), F32),
            jax.ShapeDtypeStruct(w_group.shape, F32),
            jax.ShapeDtypeStruct((chans, chans), F32),
        ),
        in_specs=[pl.BlockSpec(memory_space=pltpu.HBM)] * 5,
        out_specs=(hbm,) * 5,
        scratch_shapes=[
            *staged,
            dma((5,)),
            pltpu.VMEM((chans, cells), BF),
            *(pltpu.VMEM(one.shape, BF) for one in (inputs, w_in, w_group, w_out, cotangent)),
            dma((5,)),
            pltpu.VMEM((2, rows + 2, cross + 2, depth, chans), BF),
            pltpu.VMEM((2, rows + 2, cross + 2, depth, 3 * chans), BF),
            pltpu.VMEM((3, 9 * chans, chans), BF),
            pltpu.VMEM((3, chans, 9 * chans), BF),
            pltpu.VMEM((cells, chans), F32),
            pltpu.VMEM((cells, chans), F32),
            pltpu.VMEM((chans // GW, GW, chans), F32),
            *(
                pltpu.VMEM((count, depth_of * slab[0], chans), BF)
                for depth_of in (2, 1)
                for count in (na, na, nb, na)
            ),
            dma((2, 8)),
            dma((2, 8)),
            dma((2, na)),
            dma((2, na)),
            dma((2, nb)),
            dma((2, nb)),
            dma((2, na)),
            dma((2, na)),
        ],
        compiler_params=pltpu.CompilerParams(
            collective_id=0, has_side_effects=True, vmem_limit_bytes=64137 * 1024
        ),
    )(inputs, w_in, w_group, w_out, cotangent)
    return pl.pallas_call(
        store,
        out_shape=tuple(jax.ShapeDtypeStruct(one.shape, one.dtype) for one in results),
        in_specs=[hbm] * 5,
        out_specs=(pl.BlockSpec(memory_space=pltpu.HBM),) * 5,
        scratch_shapes=[*staged, dma((5,)), dma((5,))],
        compiler_params=pltpu.CompilerParams(vmem_limit_bytes=64137 * 1024),
    )(*results)


def solution(mesh):
    ni, nc = mesh.shape["inline"], mesh.shape["chan"]
    cfg = (ni, nc, math.gcd(ni, 4), math.gcd(nc, 2))
    field = P("inline", "chan", None, None)
    return jax.shard_map(
        functools.partial(shards, cfg),
        mesh=mesh,
        in_specs=(field, P(), P(), P(), field),
        out_specs=(field, field, P(), P(), P()),
        check_vma=False,
    )
```
